32 devices in a mesh: sec: 8 (over y, x, core), dev: 4 (over z).
Axes of the slice: x: 2, y: 2, z: 4, core: 2. Of those that a mesh axis runs over, the one named last changes fastest.
Arguments:
- rhs_interior: bfloat16 [327680, 256], P(('sec', 'dev')), may hold values from -6 to 6
- rhs_interface: float32 [10240, 256], P(('sec', 'dev')), may hold values from -6 to 6
- inv_blocks: bfloat16 [1280, 256, 256], P(('sec', 'dev')), may hold values from -0.375 to 0.375
- coupling: bfloat16 [1280, 2, 64, 256], P(('sec', 'dev')), may hold values from -0.1875 to 0.1875
- interface_map: int32 [1280, 64], P(('sec', 'dev')), may hold values from 0 to 10239, as said below
- slot_counts: int32 [1280], P(('sec', 'dev')), may hold values from 32 to 64, as said below
- column_order: int32 [256], replicated, may hold values from 0 to 255, each once
- schur_inverse: bfloat16 [10240, 10240], P('dev', 'sec'), may hold values from -0.0625 to 0.0625
Outputs:
- interior_solution: bfloat16 [327680, 256], P(('sec', 'dev'))
- interface_solution: float32 [10240, 256], P('dev')
The draws below stay inside these ranges and needn't reach their ends.
Inputs may be any that keep to these rules, and one draw needn't show every extreme that they name: `slot_counts`: every block has at least half of its 64 slots live, and some block has all 64 live. `interface_map`: split the interface rows into 32 equal ranges, range d belonging to the device of flat index d over sec+dev; of the 2560 slots of one device's blocks at most 160 point into any one range, the slots into ranges 2p and 2p + 1 together number exactly 160, and one range receives exactly 160 slots from every device.
All inputs are finite; a program needn't handle non-finite values.
Results may differ from the reference program's by a relative error of at most 0.0056.
Values may be sent and summed in bfloat16 or wider, within the bound.
A program may use at most 128 MiB of HBM per device.

```python
import jax
import jax.numpy as jnp
from jax import lax

B = 256
K = 64
NI = 10240
NBD = 40
NCOL = 256
NBLK = 1280
NU = 327680


def draw_slot_counts(key, part):
    count_key = jax.random.fold_in(key, 11)
    spot_key = jax.random.fold_in(key, 12)
    counts = jax.random.randint(count_key, (NBLK,), K // 2, K + 1)
    spot = jax.random.randint(spot_key, (), 0, NBLK)
    return counts.at[spot].set(K).astype(jnp.int32)


def draw_interface_map(key, part):
    owners = NBLK // NBD
    per_owner = NBD * K
    capacity = 2 * per_owner // owners
    piece = NI // owners
    pairs = owners // 2
    spot = jax.random.randint(jax.random.fold_in(key, 21), (), 0, pairs)
    lower = jax.random.randint(jax.random.fold_in(key, 22), (owners, pairs), capacity // 4, capacity - capacity // 4 + 1)
    lower = lower.at[:, spot].set(0)
    position = jnp.arange(capacity, dtype=jnp.int32)
    pair_index = jnp.arange(pairs, dtype=jnp.int32)
    target_owner = 2 * pair_index[None, :, None] + (position[None, None, :] >= lower[:, :, None]).astype(jnp.int32)
    target_owner = target_owner.reshape(owners, per_owner)
    shuffle_keys = jax.random.split(jax.random.fold_in(key, 23), owners)
    target_owner = jax.vmap(lambda one_key, row: jax.random.permutation(one_key, row))(shuffle_keys, target_owner)
    offsets = jax.random.randint(jax.random.fold_in(key, 24), (owners, per_owner), 0, piece)
    rows = target_owner * piece + offsets
    return rows.reshape(NBLK, K).astype(jnp.int32)


def block_scale(own_key, extent, pieces, least, high):
    gain, own = 1.0, jax.random.fold_in(own_key, 6)
    for dim, parts in pieces:
        draws = jnp.exp(jax.random.uniform(jax.random.fold_in(own, dim), (parts,), jnp.float32, least / len(pieces), high / len(pieces)))
        gain = gain * jnp.repeat(draws, extent[dim] // parts).reshape([-1 if axis == dim else 1 for axis in range(len(extent))])
    return gain


def centred(own_key, dims, width, most, cuts=(), kind=jnp.bfloat16):
    result = width * jax.random.normal(own_key, dims, jnp.float32)
    if cuts:
        result = result * block_scale(own_key, dims, cuts, -0.22, 0.18)
    return jnp.clip(result, -most, most).astype(kind)


def setup_inputs(seed: int = 0) -> dict:
    key_of = jax.random.split(jax.random.key(seed), 9)
    rhs_interior = centred(key_of[0], (NU, NCOL), 1.0, 6.0, ((0, 32),))
    rhs_interface = centred(key_of[1], (NI, NCOL), 1.0, 6.0, ((0, 32),), jnp.float32)
    inv_blocks = centred(key_of[2], (NBLK, B, B), B ** -0.5, 0.375, ((0, 32),))
    coupling = centred(key_of[3], (NBLK, 2, K, B), (4 * B) ** -0.5, 0.1875, ((0, 32),))
    interface_map = draw_interface_map(jax.random.fold_in(key_of[8], 71), 0)
    slot_counts = draw_slot_counts(jax.random.fold_in(key_of[8], 71), 0)
    column_order = jax.random.permutation(key_of[6], NCOL).astype(jnp.int32)
    schur_inverse = centred(key_of[7], (NI, NI), NI ** -0.5, 0.0625, ((0, 4), (1, 8)))
    return dict(rhs_interior=rhs_interior, rhs_interface=rhs_interface, inv_blocks=inv_blocks, coupling=coupling, interface_map=interface_map, slot_counts=slot_counts, column_order=column_order, schur_inverse=schur_inverse)


def reference(rhs_interior, rhs_interface, inv_blocks, coupling, interface_map, slot_counts, column_order, schur_inverse):
    live_mask = (jnp.arange(K, dtype=jnp.int32)[None, :] < slot_counts[:, None]).astype(jnp.float32)
    rhs_cols = jnp.take(rhs_interface, column_order, axis=1)
    groups = NBLK // NBD
    rhs_groups = rhs_interior.reshape(groups, NBD, B, NCOL)
    inv_groups = inv_blocks.reshape(groups, NBD, B, B)
    coupling_groups = coupling.reshape(groups, NBD, 2, K, B)
    map_groups = interface_map.reshape(groups, NBD * K)
    mask_groups = live_mask.reshape(groups, NBD, K)

    def forward(running, inputs):
        rhs_part, inv_part, coupling_part, map_part, mask_part = inputs
        solved = jnp.einsum("bij,bjn->bin", inv_part.astype(jnp.float32), rhs_part.astype(jnp.float32)).astype(jnp.bfloat16)
        solved = lax.optimization_barrier(solved)
        partials = jnp.einsum("bkr,brn->bkn", coupling_part[:, 0].astype(jnp.float32), solved.astype(jnp.float32))
        partials = partials * mask_part[:, :, None]
        running = running.at[map_part].add(-partials.reshape(NBD * K, NCOL))
        return running, solved

    scattered, solved_all = lax.scan(forward, jnp.zeros((NI, NCOL), jnp.float32), (rhs_groups, inv_groups, coupling_groups, map_groups, mask_groups))
    reduced = rhs_cols + scattered
    reduced_bf = reduced.astype(jnp.bfloat16)
    interface_solution = jnp.dot(schur_inverse, reduced_bf, preferred_element_type=jnp.float32)
    values = lax.optimization_barrier(interface_solution.astype(jnp.bfloat16))

    def backward(inputs):
        solved, inv_part, coupling_part, map_part, mask_part = inputs
        picked = jnp.take(values, map_part, axis=0).reshape(NBD, K, NCOL) * mask_part[:, :, None].astype(jnp.bfloat16)
        pushed = jnp.einsum("bkr,bkn->brn", coupling_part[:, 1].astype(jnp.float32), picked.astype(jnp.float32)).astype(jnp.bfloat16)
        pushed = lax.optimization_barrier(pushed)
        back_term = jnp.einsum("bij,bjn->bin", inv_part.astype(jnp.float32), pushed.astype(jnp.float32))
        return (solved.astype(jnp.float32) - back_term).astype(jnp.bfloat16)

    interior = lax.map(backward, (solved_all, inv_groups, coupling_groups, map_groups, mask_groups))
    return interior.reshape(NU, NCOL), interface_solution
```

```python
import functools
import math

import jax
import jax.numpy as jnp
from jax import lax
from jax.experimental import pallas as pl
from jax.experimental.pallas import tpu as pltpu
from jax.sharding import PartitionSpec as P

MESH = pl.DeviceIdType.MESH
F32 = jnp.float32
BF16 = jnp.bfloat16
VMEM_LIMIT = 56 * 1024 * 1024


def sort_kernel(place_ref, local_ref, rows_ref, sorted_ref, ids_ref):
    count, total = sorted_ref.shape[0], place_ref.shape[1]
    wanted = lax.broadcasted_iota(jnp.int32, (count, total), 0) + pl.program_id(0) * count
    hot = jnp.where(place_ref[...] == wanted, 1.0, 0.0).astype(BF16)
    sorted_ref[...] = jnp.dot(hot, rows_ref[...], preferred_element_type=F32).astype(BF16)
    ids_ref[...] = lax.dot_general(
        local_ref[...], hot, (((1,), (1,)), ((), ())), preferred_element_type=F32
    )[None]


def interface_kernel(
    S, D, C, PR, G,
    send_ref, ids_ref, rhs_ref, schur_ref,
    values_ref, picked_ref,
    recv, ids_recv, acc, zsend, zrecv, red, psend, precv, band, zval, gsend, picked,
    s_a, r_a, s_i, r_i, s_z, r_z, s_g, r_g, s_p, r_p, s_v, r_v, s_w, r_w, s_f, r_f, s_k, r_k, s_o,
):
    me_s, me_d = lax.axis_index("sec"), lax.axis_index("dev")
    half = PR // 2
    GC, GP = G * C, G * PR
    parity = lax.rem(me_s, 2)
    mate = me_s + 1 - 2 * parity
    quarter = me_s // 2

    def at_sec(i):
        return lax.rem(me_s + i, S)

    def at_dev(i):
        return lax.rem(me_d + i, D)

    def copy(src, dst, send, recv_sem, sec, dev):
        return pltpu.make_async_remote_copy(
            src_ref=src, dst_ref=dst, send_sem=send, recv_sem=recv_sem,
            device_id=(sec, dev), device_id_type=MESH,
        )

    barrier = pltpu.get_barrier_semaphore()
    for i in range(1, S):
        pl.semaphore_signal(barrier, inc=1, device_id=(at_sec(i), me_d), device_id_type=MESH)
    for i in range(1, D):
        pl.semaphore_signal(barrier, inc=1, device_id=(me_s, at_dev(i)), device_id_type=MESH)
    pl.semaphore_wait(barrier, S + D - 2)

    def ids_copy(i):
        return copy(ids_ref.at[at_sec(i)], ids_recv.at[i], s_i.at[i], r_i.at[i], at_sec(i), me_d)

    def a_copy(i):
        return copy(send_ref.at[at_sec(i)], recv.at[i], s_a.at[i], r_a.at[i], at_sec(i), me_d)

    def z_copy(i):
        return copy(zsend.at[i], zrecv.at[i], s_z.at[i], r_z.at[i], me_s, at_dev(i))

    def g_copy(i):
        return copy(red.at[me_d], red.at[me_d], s_g.at[i], r_g.at[i], me_s, at_dev(i))

    def p_copy(i):
        return copy(psend.at[i], precv.at[i], s_p.at[i], r_p.at[i], at_sec(i), me_d)

    def v_copy(i):
        return copy(band.at[me_s], band.at[me_s], s_v.at[i], r_v.at[i], at_sec(i), me_d)

    def w_copy(i):
        return copy(band.at[me_s], zval.at[me_d, parity], s_w.at[i], r_w.at[i], me_s, at_dev(i))

    def f_copy(i):
        from_dev = lax.rem(me_d - i + D, D)
        src = band.at[me_s] if i == 0 else zval.at[from_dev, parity]
        return copy(src, zval.at[from_dev, parity], s_f.at[i], r_f.at[i], mate, me_d)

    def k_copy(t):
        return copy(gsend.at[t], picked.at[quarter], s_k.at[t], r_k.at[t], at_sec(2 * t), me_d)

    for i in range(1, S):
        ids_copy(i).start()
        a_copy(i).start()

    def add_slots(rows, ids, first):
        for g in range(D // 2 // G):
            hot = jnp.where(
                lax.broadcasted_iota(jnp.int32, (GP, GC), 0) == ids[g : g + 1, :GC], 1.0, 0.0
            ).astype(BF16)
            part = jnp.dot(hot, rows[g * GC : (g + 1) * GC, :], preferred_element_type=F32)
            if first:
                acc[g * GP : (g + 1) * GP, :] = part
            else:
                acc[g * GP : (g + 1) * GP, :] += part

    add_slots(send_ref.at[me_s], ids_ref.at[me_s], True)

    for i in range(1, S):
        ids_copy(i).wait_recv()
        a_copy(i).wait_recv()
        add_slots(recv.at[i], ids_recv.at[i], False)

    def piece(j):
        return acc[pl.ds(pl.multiple_of(j * half, 16), half), :]

    for i in range(1, D):
        zsend[i] = piece(at_dev(i)).astype(BF16)
        z_copy(i).start()
    total = piece(me_d) + rhs_ref[...]
    for i in range(1, D):
        z_copy(i).wait_recv()
        total = total + zrecv[i].astype(F32)
    red[me_d] = total.astype(BF16)
    for i in range(1, D):
        g_copy(i).start()
    for i in range(1, D):
        g_copy(i).wait_recv()

    whole = red[...].reshape(D * half, red.shape[2])

    def product(k):
        rows = schur_ref[pl.ds(pl.multiple_of(k * half, 16), half), :]
        return jnp.dot(rows, whole, preferred_element_type=F32)

    for i in range(1, S):
        psend[i] = product(at_sec(i)).astype(BF16)
        p_copy(i).start()
    total = product(me_s)
    for i in range(1, S):
        p_copy(i).wait_recv()
        total = total + precv[i].astype(F32)
    value = total.astype(BF16)
    band[me_s] = value
    zval[me_d, parity] = value
    f_copy(0).start()
    for i in range(1, D):
        w_copy(i).start()
    for i in range(1, S):
        v_copy(i).start()
    for i in range(1, D):
        w_copy(i).wait_recv()
        f_copy(i).start()
    for i in range(D):
        f_copy(i).wait_recv()

    def gather(ids, put):
        for g in range(D // G):
            hot = jnp.where(
                lax.broadcasted_iota(jnp.int32, (GP, GC), 0) == ids[8 + g : 9 + g, :GC], 1.0, 0.0
            ).astype(BF16)
            rows = zval[g * G : (g + 1) * G].reshape(GP, zval.shape[3])
            got = lax.dot_general(
                hot, rows, (((0,), (0,)), ((), ())), preferred_element_type=F32
            )
            put(g, got.astype(BF16))

    for t in range(1, S // 2):
        def put(g, got, t=t):
            gsend[t, g * GC : (g + 1) * GC, :] = got

        gather(ids_recv.at[S - 2 * t], put)
        k_copy(t).start()

    def put_own(g, got):
        picked[quarter, g * GC : (g + 1) * GC, :] = got

    gather(ids_ref.at[me_s], put_own)

    for i in range(1, S):
        v_copy(i).wait_recv()
    out_values = pltpu.make_async_copy(band, values_ref, s_o.at[0])
    out_values.start()
    for t in range(1, S // 2):
        k_copy(t).wait_recv()
    out_picked = pltpu.make_async_copy(picked, picked_ref, s_o.at[1])
    out_picked.start()
    for i in range(1, S):
        ids_copy(i).wait_send()
        a_copy(i).wait_send()
        p_copy(i).wait_send()
        v_copy(i).wait_send()
    for i in range(1, D):
        z_copy(i).wait_send()
        g_copy(i).wait_send()
        w_copy(i).wait_send()
    for i in range(D):
        f_copy(i).wait_send()
    for t in range(1, S // 2):
        k_copy(t).wait_send()
    out_values.wait()
    out_picked.wait()


def place_kernel(place_ref, picked_ref, out_ref):
    count, total = place_ref.shape[0], picked_ref.shape[0]
    hot = jnp.where(
        place_ref[...] == lax.broadcasted_iota(jnp.int32, (count, total), 1), 1.0, 0.0
    ).astype(BF16)
    out_ref[...] = jnp.dot(hot, picked_ref[...], preferred_element_type=F32).astype(BF16)


def shards(
    rhs_interior, rhs_interface, inv_blocks, coupling, interface_map, slot_counts, column_order, schur_inverse
):
    NB, B = inv_blocks.shape[:2]
    K = coupling.shape[2]
    N = rhs_interior.shape[1]
    S, D = lax.axis_size("sec"), lax.axis_size("dev")
    rows_all = schur_inverse.shape[0] * D
    NP = S * D // 2
    PR = rows_all // NP
    slots = NB * K
    C = slots // NP
    G = 16 // math.gcd(16, C)
    GC = G * C
    L = -(-GC // 128) * 128
    half = PR // 2

    live = jnp.arange(K, dtype=jnp.int32)[None, :] < slot_counts[:, None]
    pair = interface_map // PR
    mine = pair[:, :, None] == jnp.arange(NP, dtype=jnp.int32)[None, None, :]
    hot = mine.astype(BF16)
    upto = jnp.tril(jnp.ones((K, K), BF16))
    within = jnp.einsum("kl,blp->bkp", upto, hot, preferred_element_type=F32)
    before = jnp.dot(
        jnp.tril(jnp.ones((NB, NB), BF16), -1), within[:, -1, :].astype(BF16), preferred_element_type=F32
    )
    rank = jnp.sum(jnp.where(mine, within + before[:, None, :], 0.0), axis=2).astype(jnp.int32) - 1
    local = interface_map - pair * PR
    place_a = pair * C + rank
    place_c = ((pair % (S // 2)) * D + pair // (S // 2)) * C + rank
    place_c = jnp.where(live, place_c, -1).reshape(slots, 1)
    digits = jnp.stack([local // 128, local % 128]).reshape(2, slots).astype(BF16)
    digits = jnp.pad(digits, ((0, 14), (0, 0)))

    solved = jnp.einsum(
        "bij,bjn->bin", inv_blocks, rhs_interior.reshape(NB, B, N), preferred_element_type=F32
    ).astype(BF16)
    partials = jnp.einsum("bkr,brn->bkn", coupling[:, 0], solved, preferred_element_type=F32)
    partials = jnp.where(live[:, :, None], -partials, 0.0).astype(BF16).reshape(slots, N)

    step = slots // S
    full = lambda *shape: pl.BlockSpec(shape, lambda i: (0,) * len(shape))
    ordered, id_digits = pl.pallas_call(
        sort_kernel,
        grid=(S,),
        in_specs=[full(1, slots), full(16, slots), full(slots, N)],
        out_specs=[
            pl.BlockSpec((step, N), lambda i: (i, 0)),
            pl.BlockSpec((1, 16, step), lambda i: (i, 0, 0)),
        ],
        out_shape=[
            jax.ShapeDtypeStruct((slots, N), BF16),
            jax.ShapeDtypeStruct((S, 16, step), F32),
        ],
        compiler_params=pltpu.CompilerParams(vmem_limit_bytes=VMEM_LIMIT),
    )(place_a.reshape(1, slots), digits, partials)
    ids = (id_digits[:, 0] * 128.0 + id_digits[:, 1]).astype(jnp.int32).reshape(NP, C)
    ids_a = ids.reshape(S, D // 2 // G, G, C) + (jnp.arange(G, dtype=jnp.int32) * PR)[None, None, :, None]
    ids_c = ids.reshape(D // G, G, S // 2, C) + (jnp.arange(G, dtype=jnp.int32) * PR)[None, :, None, None]
    ids_a = jnp.pad(ids_a.reshape(S, D // 2 // G, GC), ((0, 0), (0, 8 - D // 2 // G), (0, L - GC)))
    ids_c = jnp.transpose(ids_c, (2, 0, 1, 3)).reshape(S // 2, D // G, GC)
    ids_c = jnp.repeat(jnp.pad(ids_c, ((0, 0), (0, 8 - D // G), (0, L - GC))), 2, axis=0)
    ids_all = jnp.concatenate([ids_a, ids_c], axis=1)

    rhs_cols = jnp.take(rhs_interface, column_order, axis=1)

    vm = pl.BlockSpec(memory_space=pltpu.VMEM)
    anyspace = pl.BlockSpec(memory_space=pl.ANY)
    dma = pltpu.SemaphoreType.DMA
    values, picked = pl.pallas_call(
        functools.partial(interface_kernel, S, D, C, PR, G),
        in_specs=[vm] * 4,
        out_specs=[anyspace] * 2,
        out_shape=[
            jax.ShapeDtypeStruct((S, half, N), BF16),
            jax.ShapeDtypeStruct((S // 2, D * C, N), BF16),
        ],
        scratch_shapes=[
            pltpu.VMEM((S, D // 2 * C, N), BF16),
            pltpu.VMEM((S, 16, L), jnp.int32),
            pltpu.VMEM((D * half, N), F32),
            pltpu.VMEM((D, half, N), BF16),
            pltpu.VMEM((D, half, N), BF16),
            pltpu.VMEM((D, half, N), BF16),
            pltpu.VMEM((S, half, N), BF16),
            pltpu.VMEM((S, half, N), BF16),
            pltpu.VMEM((S, half, N), BF16),
            pltpu.VMEM((D, 2, half, N), BF16),
            pltpu.VMEM((S // 2, D * C, N), BF16),
            pltpu.VMEM((S // 2, D * C, N), BF16),
            dma((S,)), dma((S,)), dma((S,)), dma((S,)), dma((D,)), dma((D,)), dma((D,)), dma((D,)),
            dma((S,)), dma((S,)), dma((S,)), dma((S,)), dma((D,)), dma((D,)), dma((D,)), dma((D,)),
            dma((S // 2,)), dma((S // 2,)), dma((2,)),
        ],
        compiler_params=pltpu.CompilerParams(
            collective_id=0, has_side_effects=True, vmem_limit_bytes=VMEM_LIMIT
        ),
    )(ordered.reshape(S, step, N), ids_all, rhs_cols, schur_inverse)

    interface_solution = values.reshape(S * half, N).astype(F32)
    picked = pl.pallas_call(
        place_kernel,
        grid=(S,),
        in_specs=[pl.BlockSpec((step, 1), lambda i: (i, 0)), full(slots, N)],
        out_specs=pl.BlockSpec((step, N), lambda i: (i, 0)),
        out_shape=jax.ShapeDtypeStruct((slots, N), BF16),
        compiler_params=pltpu.CompilerParams(vmem_limit_bytes=VMEM_LIMIT),
    )(place_c, picked.reshape(slots, N)).reshape(NB, K, N)

    pushed = jnp.einsum("bkr,bkn->brn", coupling[:, 1], picked, preferred_element_type=F32).astype(BF16)
    back_term = jnp.einsum("bij,bjn->bin", inv_blocks, pushed, preferred_element_type=F32)
    interior = (solved.astype(F32) - back_term).astype(BF16)
    return (interior.reshape(NB * B, N), interface_solution)


def solution(mesh):
    placed = (
        P(("sec", "dev"), None),
        P(("sec", "dev"), None),
        P(("sec", "dev"), None, None),
        P(("sec", "dev"), None, None, None),
        P(("sec", "dev"), None),
        P(("sec", "dev")),
        P(),
        P("dev", "sec"),
    )
    return jax.shard_map(
        shards,
        mesh=mesh,
        in_specs=placed,
        out_specs=(P(("sec", "dev"), None), P("dev", None)),
        check_vma=False,
    )
```

```python
import functools
import math

import jax
import jax.numpy as jnp
from jax import lax
from jax.experimental import pallas as pl
from jax.experimental.pallas import tpu as pltpu
from jax.sharding import PartitionSpec as P

MESH = pl.DeviceIdType.MESH
F32 = jnp.float32
BF16 = jnp.bfloat16
VMEM_LIMIT = 56 * 1024 * 1024
PARTS = 2


def sort_kernel(place_ref, local_ref, rows_ref, sorted_ref, ids_ref):
    count, total = sorted_ref.shape[0], place_ref.shape[1]
    wanted = lax.broadcasted_iota(jnp.int32, (count, total), 0) + pl.program_id(0) * count
    hot = jnp.where(place_ref[...] == wanted, 1.0, 0.0).astype(BF16)
    sorted_ref[...] = jnp.dot(hot, rows_ref[...], preferred_element_type=F32).astype(BF16)
    ids_ref[...] = lax.dot_general(
        local_ref[...], hot, (((1,), (1,)), ((), ())), preferred_element_type=F32
    )[None]


def interface_kernel(
    S, D, C, PR, G,
    send_ref, ids_ref, rhs_ref, schur_ref,
    values_ref, picked_ref,
    recv, ids_recv, acc, zsend, zrecv, red, own, msend, mrecv, psend, precv, band, zval, gsend, picked,
    s_i, r_i, s_a, r_a, s_z, r_z, s_g, r_g, s_m, r_m, s_p, r_p, s_v, r_v, s_u, r_u, s_w, r_w, s_f, r_f, s_k, r_k, s_o,
):
    me_s, me_d = lax.axis_index("sec"), lax.axis_index("dev")
    half = PR // 2
    Q = S // 2
    GC, GP = G * C, G * PR
    parity = lax.rem(me_s, 2)
    mate = me_s + 1 - 2 * parity
    quarter = me_s // 2
    width = rhs_ref.shape[1] // PARTS
    parts = range(PARTS)

    def cols(h):
        return pl.ds(h * width, width)

    def at_sec(i):
        return lax.rem(me_s + i, S)

    def at_dev(i):
        return lax.rem(me_d + i, D)

    def copy(src, dst, send, recv_sem, sec, dev):
        return pltpu.make_async_remote_copy(
            src_ref=src, dst_ref=dst, send_sem=send, recv_sem=recv_sem,
            device_id=(sec, dev), device_id_type=MESH,
        )

    barrier = pltpu.get_barrier_semaphore()
    for i in range(1, S):
        pl.semaphore_signal(barrier, inc=1, device_id=(at_sec(i), me_d), device_id_type=MESH)
    for i in range(1, D):
        pl.semaphore_signal(barrier, inc=1, device_id=(me_s, at_dev(i)), device_id_type=MESH)
    pl.semaphore_wait(barrier, S + D - 2)

    def ids_copy(i):
        return copy(ids_ref.at[at_sec(i)], ids_recv.at[i], s_i.at[i], r_i.at[i], at_sec(i), me_d)

    def part_copy(src, dst, h, i, send, recv_sem, sec, dev):
        return copy(src.at[:, cols(h)], dst.at[:, cols(h)], send.at[h, i], recv_sem.at[h, i], sec, dev)

    def a_copy(h, i):
        return part_copy(send_ref.at[at_sec(i)], recv.at[i], h, i, s_a, r_a, at_sec(i), me_d)

    def z_copy(h, i):
        return part_copy(zsend.at[i], zrecv.at[i], h, i, s_z, r_z, me_s, at_dev(i))

    def g_copy(h, i):
        return part_copy(red.at[me_d], red.at[me_d], h, i, s_g, r_g, me_s, at_dev(i))

    def m_copy(h, t):
        return part_copy(msend.at[t], mrecv.at[t], h, t, s_m, r_m, mate, me_d)

    def p_copy(h, t):
        return part_copy(psend.at[t], precv.at[t], h, t, s_p, r_p, at_sec(2 * t), me_d)

    def v_copy(h, t):
        return part_copy(band.at[me_s], band.at[me_s], h, t, s_v, r_v, at_sec(2 * t), me_d)

    def u_copy(h, t):
        k = lax.rem(me_s - 2 * t + S, S)
        return part_copy(band.at[k], band.at[k], h, t, s_u, r_u, mate, me_d)

    def w_copy(h, i):
        return part_copy(band.at[me_s], zval.at[me_d, parity], h, i, s_w, r_w, me_s, at_dev(i))

    def f_copy(h, i):
        k = lax.rem(me_d - i + D, D)
        src = band.at[me_s] if i == 0 else zval.at[k, parity]
        return part_copy(src, zval.at[k, parity], h, i, s_f, r_f, mate, me_d)

    def k_copy(h, t):
        return part_copy(gsend.at[t], picked.at[quarter], h, t, s_k, r_k, at_sec(2 * t), me_d)

    for i in range(1, S):
        ids_copy(i).start()
    for h in parts:
        for i in range(1, S):
            a_copy(h, i).start()

    def add_slots(rows, ids, h, first):
        for g in range(D // 2 // G):
            hot = jnp.where(
                lax.broadcasted_iota(jnp.int32, (GP, GC), 0) == ids[g : g + 1, :GC], 1.0, 0.0
            ).astype(BF16)
            part = jnp.dot(hot, rows[g * GC : (g + 1) * GC, cols(h)], preferred_element_type=F32)
            if first:
                acc[g * GP : (g + 1) * GP, cols(h)] = part
            else:
                acc[g * GP : (g + 1) * GP, cols(h)] += part

    def piece(j, h):
        return acc[pl.ds(pl.multiple_of(j * half, 16), half), cols(h)]

    for h in parts:
        add_slots(send_ref.at[me_s], ids_ref.at[me_s], h, True)
    for h in parts:
        for i in range(1, S):
            if h == 0:
                ids_copy(i).wait_recv()
            a_copy(h, i).wait_recv()
            add_slots(recv.at[i], ids_recv.at[i], h, False)
        for i in range(1, D):
            zsend[i, :, cols(h)] = piece(at_dev(i), h).astype(BF16)
            z_copy(h, i).start()
    for h in parts:
        total = piece(me_d, h) + rhs_ref[:, cols(h)]
        for i in range(1, D):
            z_copy(h, i).wait_recv()
            total = total + zrecv[i, :, cols(h)].astype(F32)
        red[me_d, :, cols(h)] = total.astype(BF16)
        for i in range(1, D):
            g_copy(h, i).start()

    for h in parts:
        for i in range(1, D):
            g_copy(h, i).wait_recv()
        whole = red[:, :, cols(h)].reshape(D * half, width)

        def product(k):
            rows = schur_ref[pl.ds(pl.multiple_of(k * half, 16), half), :]
            return jnp.dot(rows, whole, preferred_element_type=F32)

        order = [*range(1, Q), 0]
        for t in order:
            msend[t, :, cols(h)] = product(lax.rem(mate + 2 * t, S)).astype(BF16)
            m_copy(h, t).start()
        for t in order:
            total = product(at_sec(2 * t))
            m_copy(h, t).wait_recv()
            total = total + mrecv[t, :, cols(h)].astype(F32)
            if t:
                psend[t, :, cols(h)] = total.astype(BF16)
                p_copy(h, t).start()
            else:
                own[:, cols(h)] = total
    for h in parts:
        total = own[:, cols(h)]
        for t in range(1, Q):
            p_copy(h, t).wait_recv()
            total = total + precv[t, :, cols(h)].astype(F32)
        value = total.astype(BF16)
        band[me_s, :, cols(h)] = value
        zval[me_d, parity, :, cols(h)] = value
        f_copy(h, 0).start()
        for i in range(1, D):
            w_copy(h, i).start()
        for t in range(1, Q):
            v_copy(h, t).start()

    def gather(ids, h, put):
        for g in range(D // G):
            hot = jnp.where(
                lax.broadcasted_iota(jnp.int32, (GP, GC), 0) == ids[8 + g : 9 + g, :GC], 1.0, 0.0
            ).astype(BF16)
            rows = zval[g * G : (g + 1) * G, :, :, cols(h)].reshape(GP, width)
            got = lax.dot_general(
                hot, rows, (((0,), (0,)), ((), ())), preferred_element_type=F32
            )
            put(g, got.astype(BF16))

    for h in parts:
        for i in range(1, D):
            w_copy(h, i).wait_recv()
            f_copy(h, i).start()
        for i in range(D):
            f_copy(h, i).wait_recv()
        for t in range(1, Q):
            def put(g, got):
                gsend[t, g * GC : (g + 1) * GC, cols(h)] = got

            gather(ids_recv.at[S - 2 * t], h, put)
            k_copy(h, t).start()
        for t in range(1, Q):
            v_copy(h, t).wait_recv()
            u_copy(h, t).start()

    for h in parts:
        def put_own(g, got):
            picked[quarter, g * GC : (g + 1) * GC, cols(h)] = got

        gather(ids_ref.at[me_s], h, put_own)
        band[mate, :, cols(h)] = zval[me_d, 1 - parity, :, cols(h)]
    for h in parts:
        for t in range(1, Q):
            u_copy(h, t).wait_recv()
    out_values = pltpu.make_async_copy(band, values_ref, s_o.at[0])
    out_values.start()
    for h in parts:
        for t in range(1, Q):
            k_copy(h, t).wait_recv()
    out_picked = pltpu.make_async_copy(picked, picked_ref, s_o.at[1])
    out_picked.start()
    for i in range(1, S):
        ids_copy(i).wait_send()
    for h in parts:
        for i in range(1, S):
            a_copy(h, i).wait_send()
        for i in range(1, D):
            z_copy(h, i).wait_send()
            g_copy(h, i).wait_send()
            w_copy(h, i).wait_send()
        for i in range(D):
            f_copy(h, i).wait_send()
        for t in range(Q):
            m_copy(h, t).wait_send()
        for t in range(1, Q):
            p_copy(h, t).wait_send()
            v_copy(h, t).wait_send()
            u_copy(h, t).wait_send()
            k_copy(h, t).wait_send()
    out_values.wait()
    out_picked.wait()


def place_kernel(place_ref, picked_ref, out_ref):
    count, total = place_ref.shape[0], picked_ref.shape[0]
    hot = jnp.where(
        place_ref[...] == lax.broadcasted_iota(jnp.int32, (count, total), 1), 1.0, 0.0
    ).astype(BF16)
    out_ref[...] = jnp.dot(hot, picked_ref[...], preferred_element_type=F32).astype(BF16)


def shards(
    rhs_interior, rhs_interface, inv_blocks, coupling, interface_map, slot_counts, column_order, schur_inverse
):
    NB, B = inv_blocks.shape[:2]
    K = coupling.shape[2]
    N = rhs_interior.shape[1]
    S, D = lax.axis_size("sec"), lax.axis_size("dev")
    rows_all = schur_inverse.shape[0] * D
    NP = S * D // 2
    PR = rows_all // NP
    slots = NB * K
    C = slots // NP
    G = 16 // math.gcd(16, C)
    GC = G * C
    L = -(-GC // 128) * 128
    half = PR // 2

    live = jnp.arange(K, dtype=jnp.int32)[None, :] < slot_counts[:, None]
    pair = interface_map // PR
    mine = pair[:, :, None] == jnp.arange(NP, dtype=jnp.int32)[None, None, :]
    hot = mine.astype(BF16)
    upto = jnp.tril(jnp.ones((K, K), BF16))
    within = jnp.einsum("kl,blp->bkp", upto, hot, preferred_element_type=F32)
    before = jnp.dot(
        jnp.tril(jnp.ones((NB, NB), BF16), -1), within[:, -1, :].astype(BF16), preferred_element_type=F32
    )
    rank = jnp.sum(jnp.where(mine, within + before[:, None, :], 0.0), axis=2).astype(jnp.int32) - 1
    local = interface_map - pair * PR
    place_a = pair * C + rank
    place_c = ((pair % (S // 2)) * D + pair // (S // 2)) * C + rank
    place_c = jnp.where(live, place_c, -1).reshape(slots, 1)
    digits = jnp.stack([local // 128, local % 128]).reshape(2, slots).astype(BF16)
    digits = jnp.pad(digits, ((0, 14), (0, 0)))

    solved = jnp.einsum(
        "bij,bjn->bin", inv_blocks, rhs_interior.reshape(NB, B, N), preferred_element_type=F32
    ).astype(BF16)
    partials = jnp.einsum("bkr,brn->bkn", coupling[:, 0], solved, preferred_element_type=F32)
    partials = jnp.where(live[:, :, None], -partials, 0.0).astype(BF16).reshape(slots, N)

    step = slots // S
    full = lambda *shape: pl.BlockSpec(shape, lambda i: (0,) * len(shape))
    ordered, id_digits = pl.pallas_call(
        sort_kernel,
        grid=(S,),
        in_specs=[full(1, slots), full(16, slots), full(slots, N)],
        out_specs=[
            pl.BlockSpec((step, N), lambda i: (i, 0)),
            pl.BlockSpec((1, 16, step), lambda i: (i, 0, 0)),
        ],
        out_shape=[
            jax.ShapeDtypeStruct((slots, N), BF16),
            jax.ShapeDtypeStruct((S, 16, step), F32),
        ],
        compiler_params=pltpu.CompilerParams(vmem_limit_bytes=VMEM_LIMIT),
    )(place_a.reshape(1, slots), digits, partials)
    ids = (id_digits[:, 0] * 128.0 + id_digits[:, 1]).astype(jnp.int32).reshape(NP, C)
    ids_a = ids.reshape(S, D // 2 // G, G, C) + (jnp.arange(G, dtype=jnp.int32) * PR)[None, None, :, None]
    ids_c = ids.reshape(D // G, G, S // 2, C) + (jnp.arange(G, dtype=jnp.int32) * PR)[None, :, None, None]
    ids_a = jnp.pad(ids_a.reshape(S, D // 2 // G, GC), ((0, 0), (0, 8 - D // 2 // G), (0, L - GC)))
    ids_c = jnp.transpose(ids_c, (2, 0, 1, 3)).reshape(S // 2, D // G, GC)
    ids_c = jnp.repeat(jnp.pad(ids_c, ((0, 0), (0, 8 - D // G), (0, L - GC))), 2, axis=0)
    ids_all = jnp.concatenate([ids_a, ids_c], axis=1)

    rhs_cols = jnp.take(rhs_interface, column_order, axis=1)

    vm = pl.BlockSpec(memory_space=pltpu.VMEM)
    anyspace = pl.BlockSpec(memory_space=pl.ANY)
    dma = pltpu.SemaphoreType.DMA
    values, picked = pl.pallas_call(
        functools.partial(interface_kernel, S, D, C, PR, G),
        in_specs=[vm] * 4,
        out_specs=[anyspace] * 2,
        out_shape=[
            jax.ShapeDtypeStruct((S, half, N), BF16),
            jax.ShapeDtypeStruct((S // 2, D * C, N), BF16),
        ],
        scratch_shapes=[
            pltpu.VMEM((S, D // 2 * C, N), BF16),
            pltpu.VMEM((S, 16, L), jnp.int32),
            pltpu.VMEM((D * half, N), F32),
            pltpu.VMEM((D, half, N), BF16),
            pltpu.VMEM((D, half, N), BF16),
            pltpu.VMEM((D, half, N), BF16),
            pltpu.VMEM((half, N), F32),
            *[pltpu.VMEM((S // 2, half, N), BF16)] * 4,
            pltpu.VMEM((S, half, N), BF16),
            pltpu.VMEM((D, 2, half, N), BF16),
            pltpu.VMEM((S // 2, D * C, N), BF16),
            pltpu.VMEM((S // 2, D * C, N), BF16),
            dma((S,)), dma((S,)),
            *[dma((PARTS, S))] * 2,
            *[dma((PARTS, D))] * 4,
            *[dma((PARTS, S // 2))] * 8,
            *[dma((PARTS, D))] * 4,
            *[dma((PARTS, S // 2))] * 2,
            dma((2,)),
        ],
        compiler_params=pltpu.CompilerParams(
            collective_id=0, has_side_effects=True, vmem_limit_bytes=VMEM_LIMIT
        ),
    )(ordered.reshape(S, step, N), ids_all, rhs_cols, schur_inverse)

    interface_solution = values.reshape(S * half, N).astype(F32)
    picked = pl.pallas_call(
        place_kernel,
        grid=(S,),
        in_specs=[pl.BlockSpec((step, 1), lambda i: (i, 0)), full(slots, N)],
        out_specs=pl.BlockSpec((step, N), lambda i: (i, 0)),
        out_shape=jax.ShapeDtypeStruct((slots, N), BF16),
        compiler_params=pltpu.CompilerParams(vmem_limit_bytes=VMEM_LIMIT),
    )(place_c, picked.reshape(slots, N)).reshape(NB, K, N)

    pushed = jnp.einsum("bkr,bkn->brn", coupling[:, 1], picked, preferred_element_type=F32).astype(BF16)
    back_term = jnp.einsum("bij,bjn->bin", inv_blocks, pushed, preferred_element_type=F32)
    interior = (solved.astype(F32) - back_term).astype(BF16)
    return (interior.reshape(NB * B, N), interface_solution)


def solution(mesh):
    placed = (
        P(("sec", "dev"), None),
        P(("sec", "dev"), None),
        P(("sec", "dev"), None, None),
        P(("sec", "dev"), None, None, None),
        P(("sec", "dev"), None),
        P(("sec", "dev")),
        P(),
        P("dev", "sec"),
    )
    return jax.shard_map(
        shards,
        mesh=mesh,
        in_specs=placed,
        out_specs=(P(("sec", "dev"), None), P("dev", None)),
        check_vma=False,
    )
```

```python
import functools
import math

import jax
import jax.numpy as jnp
from jax import lax
from jax.experimental import pallas as pl
from jax.experimental.pallas import tpu as pltpu
from jax.sharding import PartitionSpec as P

MESH = pl.DeviceIdType.MESH
F32 = jnp.float32
BF16 = jnp.bfloat16
VMEM_LIMIT = 56 * 1024 * 1024
PARTS = 2


def sort_kernel(place_ref, local_ref, rows_ref, sorted_ref, ids_ref):
    count, total = sorted_ref.shape[0], place_ref.shape[1]
    wanted = lax.broadcasted_iota(jnp.int32, (count, total), 0) + pl.program_id(0) * count
    hot = jnp.where(place_ref[...] == wanted, 1.0, 0.0).astype(BF16)
    sorted_ref[...] = jnp.dot(hot, rows_ref[...], preferred_element_type=F32).astype(BF16)
    ids_ref[...] = lax.dot_general(
        local_ref[...], hot, (((1,), (1,)), ((), ())), preferred_element_type=F32
    )[None]


def interface_kernel(
    S, D, C, PR, G,
    send_ref, ids_ref, rhs_ref, schur_ref,
    values_ref, picked_ref,
    schur, recv, ids_recv, acc, zsend, zrecv, red, own, msend, mrecv, psend, precv, band, zval, gsend, picked,
    s_i, r_i, s_a, r_a, s_z, r_z, s_g, r_g, s_m, r_m, s_p, r_p, s_v, r_v, s_u, r_u, s_w, r_w, s_f, r_f, s_k, r_k, s_o,
):
    me_s, me_d = lax.axis_index("sec"), lax.axis_index("dev")
    half = PR // 2
    Q = S // 2
    GC, GP = G * C, G * PR
    parity = lax.rem(me_s, 2)
    mate = me_s + 1 - 2 * parity
    quarter = me_s // 2
    width = rhs_ref.shape[1] // PARTS
    parts = range(PARTS)

    def cols(h):
        return pl.ds(h * width, width)

    def at_sec(i):
        return lax.rem(me_s + i, S)

    def at_dev(i):
        return lax.rem(me_d + i, D)

    def copy(src, dst, send, recv_sem, sec, dev):
        return pltpu.make_async_remote_copy(
            src_ref=src, dst_ref=dst, send_sem=send, recv_sem=recv_sem,
            device_id=(sec, dev), device_id_type=MESH,
        )

    barrier = pltpu.get_barrier_semaphore()
    for i in range(1, S):
        pl.semaphore_signal(barrier, inc=1, device_id=(at_sec(i), me_d), device_id_type=MESH)
    for i in range(1, D):
        pl.semaphore_signal(barrier, inc=1, device_id=(me_s, at_dev(i)), device_id_type=MESH)
    pl.semaphore_wait(barrier, S + D - 2)

    def ids_copy(i):
        return copy(ids_ref.at[at_sec(i)], ids_recv.at[i], s_i.at[i], r_i.at[i], at_sec(i), me_d)

    def part_copy(src, dst, h, i, send, recv_sem, sec, dev):
        return copy(src.at[:, cols(h)], dst.at[:, cols(h)], send.at[h, i], recv_sem.at[h, i], sec, dev)

    def a_copy(h, i):
        return part_copy(send_ref.at[at_sec(i)], recv.at[i], h, i, s_a, r_a, at_sec(i), me_d)

    def z_copy(h, i):
        return part_copy(zsend.at[i], zrecv.at[i], h, i, s_z, r_z, me_s, at_dev(i))

    def g_copy(h, i):
        return part_copy(red.at[me_d], red.at[me_d], h, i, s_g, r_g, me_s, at_dev(i))

    def m_copy(h, t):
        return part_copy(msend.at[t], mrecv.at[t], h, t, s_m, r_m, mate, me_d)

    def p_copy(h, t):
        return part_copy(psend.at[t], precv.at[t], h, t, s_p, r_p, at_sec(2 * t), me_d)

    def v_copy(h, t):
        return part_copy(band.at[me_s], band.at[me_s], h, t, s_v, r_v, at_sec(2 * t), me_d)

    def u_copy(h, t):
        k = lax.rem(me_s - 2 * t + S, S)
        return part_copy(band.at[k], band.at[k], h, t, s_u, r_u, mate, me_d)

    def w_copy(h, i):
        return part_copy(band.at[me_s], zval.at[me_d, parity], h, i, s_w, r_w, me_s, at_dev(i))

    def f_copy(h, i):
        k = lax.rem(me_d - i + D, D)
        src = band.at[me_s] if i == 0 else zval.at[k, parity]
        return part_copy(src, zval.at[k, parity], h, i, s_f, r_f, mate, me_d)

    def k_copy(h, t):
        return part_copy(gsend.at[t], picked.at[quarter], h, t, s_k, r_k, at_sec(2 * t), me_d)

    for i in range(1, S):
        ids_copy(i).start()
    load = pltpu.make_async_copy(schur_ref, schur, s_o.at[2])
    load.start()
    for h in parts:
        for i in range(1, S):
            a_copy(h, i).start()

    def add_slots(rows, ids, h, first):
        for g in range(D // 2 // G):
            hot = jnp.where(
                lax.broadcasted_iota(jnp.int32, (GP, GC), 0) == ids[g : g + 1, :GC], 1.0, 0.0
            ).astype(BF16)
            part = jnp.dot(hot, rows[g * GC : (g + 1) * GC, cols(h)], preferred_element_type=F32)
            if first:
                acc[g * GP : (g + 1) * GP, cols(h)] = part
            else:
                acc[g * GP : (g + 1) * GP, cols(h)] += part

    def piece(j, h):
        return acc[pl.ds(pl.multiple_of(j * half, 16), half), cols(h)]

    for h in parts:
        add_slots(send_ref.at[me_s], ids_ref.at[me_s], h, True)
    for h in parts:
        for i in range(1, S):
            if h == 0:
                ids_copy(i).wait_recv()
            a_copy(h, i).wait_recv()
            add_slots(recv.at[i], ids_recv.at[i], h, False)
        for i in range(1, D):
            zsend[i, :, cols(h)] = piece(at_dev(i), h).astype(BF16)
            z_copy(h, i).start()
    for h in parts:
        total = piece(me_d, h) + rhs_ref[:, cols(h)]
        for i in range(1, D):
            z_copy(h, i).wait_recv()
            total = total + zrecv[i, :, cols(h)].astype(F32)
        red[me_d, :, cols(h)] = total.astype(BF16)
        for i in range(1, D):
            g_copy(h, i).start()

    load.wait()

    for h in parts:
        for i in range(1, D):
            g_copy(h, i).wait_recv()
        whole = red[:, :, cols(h)].reshape(D * half, width)

        def product(k):
            rows = schur[pl.ds(pl.multiple_of(k * half, 16), half), :]
            return jnp.dot(rows, whole, preferred_element_type=F32)

        order = [*range(1, Q), 0]
        for t in order:
            msend[t, :, cols(h)] = product(lax.rem(mate + 2 * t, S)).astype(BF16)
            m_copy(h, t).start()
        for t in order:
            total = product(at_sec(2 * t))
            m_copy(h, t).wait_recv()
            total = total + mrecv[t, :, cols(h)].astype(F32)
            if t:
                psend[t, :, cols(h)] = total.astype(BF16)
                p_copy(h, t).start()
            else:
                own[:, cols(h)] = total
    for h in parts:
        total = own[:, cols(h)]
        for t in range(1, Q):
            p_copy(h, t).wait_recv()
            total = total + precv[t, :, cols(h)].astype(F32)
        value = total.astype(BF16)
        band[me_s, :, cols(h)] = value
        zval[me_d, parity, :, cols(h)] = value
        f_copy(h, 0).start()
        for i in range(1, D):
            w_copy(h, i).start()
        for t in range(1, Q):
            v_copy(h, t).start()

    def gather(ids, h, put):
        for g in range(D // G):
            hot = jnp.where(
                lax.broadcasted_iota(jnp.int32, (GP, GC), 0) == ids[8 + g : 9 + g, :GC], 1.0, 0.0
            ).astype(BF16)
            rows = zval[g * G : (g + 1) * G, :, :, cols(h)].reshape(GP, width)
            got = lax.dot_general(
                hot, rows, (((0,), (0,)), ((), ())), preferred_element_type=F32
            )
            put(g, got.astype(BF16))

    for h in parts:
        for i in range(1, D):
            w_copy(h, i).wait_recv()
            f_copy(h, i).start()
        for i in range(D):
            f_copy(h, i).wait_recv()
        for t in range(1, Q):
            def put(g, got):
                gsend[t, g * GC : (g + 1) * GC, cols(h)] = got

            gather(ids_recv.at[S - 2 * t], h, put)
            k_copy(h, t).start()
        for t in range(1, Q):
            v_copy(h, t).wait_recv()
            u_copy(h, t).start()

    for h in parts:
        def put_own(g, got):
            picked[quarter, g * GC : (g + 1) * GC, cols(h)] = got

        gather(ids_ref.at[me_s], h, put_own)
        band[mate, :, cols(h)] = zval[me_d, 1 - parity, :, cols(h)]
    for h in parts:
        for t in range(1, Q):
            u_copy(h, t).wait_recv()
    out_values = pltpu.make_async_copy(band, values_ref, s_o.at[0])
    out_values.start()
    for h in parts:
        for t in range(1, Q):
            k_copy(h, t).wait_recv()
    out_picked = pltpu.make_async_copy(picked, picked_ref, s_o.at[1])
    out_picked.start()
    for i in range(1, S):
        ids_copy(i).wait_send()
    for h in parts:
        for i in range(1, S):
            a_copy(h, i).wait_send()
        for i in range(1, D):
            z_copy(h, i).wait_send()
            g_copy(h, i).wait_send()
            w_copy(h, i).wait_send()
        for i in range(D):
            f_copy(h, i).wait_send()
        for t in range(Q):
            m_copy(h, t).wait_send()
        for t in range(1, Q):
            p_copy(h, t).wait_send()
            v_copy(h, t).wait_send()
            u_copy(h, t).wait_send()
            k_copy(h, t).wait_send()
    out_values.wait()
    out_picked.wait()


def back_kernel(place_ref, picked_ref, coupling_ref, inv_ref, solved_ref, out_ref):
    blocks, K = coupling_ref.shape[0], coupling_ref.shape[1]
    count, total = blocks * K, picked_ref.shape[0]
    place = jnp.transpose(jnp.broadcast_to(place_ref[0], (8, count)))[:, :1].astype(jnp.int32)
    hot = jnp.where(
        place == lax.broadcasted_iota(jnp.int32, (count, total), 1), 1.0, 0.0
    ).astype(BF16)
    got = jnp.dot(hot, picked_ref[...], preferred_element_type=F32).astype(BF16)
    for b in range(blocks):
        pushed = lax.dot_general(
            coupling_ref[b], got[b * K : (b + 1) * K], (((0,), (0,)), ((), ())), preferred_element_type=F32
        ).astype(BF16)
        back = jnp.dot(inv_ref[b], pushed, preferred_element_type=F32)
        out_ref[b] = (solved_ref[b].astype(F32) - back).astype(BF16)


def shards(
    rhs_interior, rhs_interface, inv_blocks, coupling, interface_map, slot_counts, column_order, schur_inverse
):
    NB, B = inv_blocks.shape[:2]
    K = coupling.shape[2]
    N = rhs_interior.shape[1]
    S, D = lax.axis_size("sec"), lax.axis_size("dev")
    rows_all = schur_inverse.shape[0] * D
    NP = S * D // 2
    PR = rows_all // NP
    slots = NB * K
    C = slots // NP
    G = 16 // math.gcd(16, C)
    GC = G * C
    L = -(-GC // 128) * 128
    half = PR // 2

    live = jnp.arange(K, dtype=jnp.int32)[None, :] < slot_counts[:, None]
    pair = interface_map // PR
    mine = pair[:, :, None] == jnp.arange(NP, dtype=jnp.int32)[None, None, :]
    hot = mine.astype(BF16)
    upto = jnp.tril(jnp.ones((K, K), BF16))
    within = jnp.einsum("kl,blp->bkp", upto, hot, preferred_element_type=F32)
    before = jnp.dot(
        jnp.tril(jnp.ones((NB, NB), BF16), -1), within[:, -1, :].astype(BF16), preferred_element_type=F32
    )
    rank = jnp.sum(jnp.where(mine, within + before[:, None, :], 0.0), axis=2).astype(jnp.int32) - 1
    local = interface_map - pair * PR
    place_a = pair * C + rank
    place_c = ((pair % (S // 2)) * D + pair // (S // 2)) * C + rank
    place_c = jnp.where(live, place_c, -1).astype(F32)
    digits = jnp.stack([local // 128, local % 128]).reshape(2, slots).astype(BF16)
    digits = jnp.pad(digits, ((0, 14), (0, 0)))

    solved = jnp.einsum(
        "bij,bjn->bin", inv_blocks, rhs_interior.reshape(NB, B, N), preferred_element_type=F32
    ).astype(BF16)
    partials = jnp.einsum("bkr,brn->bkn", coupling[:, 0], solved, preferred_element_type=F32)
    partials = jnp.where(live[:, :, None], -partials, 0.0).astype(BF16).reshape(slots, N)

    step = slots // S
    full = lambda *shape: pl.BlockSpec(shape, lambda i: (0,) * len(shape))
    ordered, id_digits = pl.pallas_call(
        sort_kernel,
        grid=(S,),
        in_specs=[full(1, slots), full(16, slots), full(slots, N)],
        out_specs=[
            pl.BlockSpec((step, N), lambda i: (i, 0)),
            pl.BlockSpec((1, 16, step), lambda i: (i, 0, 0)),
        ],
        out_shape=[
            jax.ShapeDtypeStruct((slots, N), BF16),
            jax.ShapeDtypeStruct((S, 16, step), F32),
        ],
        compiler_params=pltpu.CompilerParams(vmem_limit_bytes=VMEM_LIMIT),
    )(place_a.reshape(1, slots), digits, partials)
    ids = (id_digits[:, 0] * 128.0 + id_digits[:, 1]).astype(jnp.int32).reshape(NP, C)
    ids_a = ids.reshape(S, D // 2 // G, G, C) + (jnp.arange(G, dtype=jnp.int32) * PR)[None, None, :, None]
    ids_c = ids.reshape(D // G, G, S // 2, C) + (jnp.arange(G, dtype=jnp.int32) * PR)[None, :, None, None]
    ids_a = jnp.pad(ids_a.reshape(S, D // 2 // G, GC), ((0, 0), (0, 8 - D // 2 // G), (0, L - GC)))
    ids_c = jnp.transpose(ids_c, (2, 0, 1, 3)).reshape(S // 2, D // G, GC)
    ids_c = jnp.repeat(jnp.pad(ids_c, ((0, 0), (0, 8 - D // G), (0, L - GC))), 2, axis=0)
    ids_all = jnp.concatenate([ids_a, ids_c], axis=1)

    rhs_cols = jnp.take(rhs_interface, column_order, axis=1)

    vm = pl.BlockSpec(memory_space=pltpu.VMEM)
    anyspace = pl.BlockSpec(memory_space=pl.ANY)
    dma = pltpu.SemaphoreType.DMA
    values, picked = pl.pallas_call(
        functools.partial(interface_kernel, S, D, C, PR, G),
        in_specs=[vm] * 3 + [anyspace],
        out_specs=[anyspace] * 2,
        out_shape=[
            jax.ShapeDtypeStruct((S, half, N), BF16),
            jax.ShapeDtypeStruct((S // 2, D * C, N), BF16),
        ],
        scratch_shapes=[
            pltpu.VMEM(schur_inverse.shape, BF16),
            pltpu.VMEM((S, D // 2 * C, N), BF16),
            pltpu.VMEM((S, 16, L), jnp.int32),
            pltpu.VMEM((D * half, N), F32),
            pltpu.VMEM((D, half, N), BF16),
            pltpu.VMEM((D, half, N), BF16),
            pltpu.VMEM((D, half, N), BF16),
            pltpu.VMEM((half, N), F32),
            *[pltpu.VMEM((S // 2, half, N), BF16)] * 4,
            pltpu.VMEM((S, half, N), BF16),
            pltpu.VMEM((D, 2, half, N), BF16),
            pltpu.VMEM((S // 2, D * C, N), BF16),
            pltpu.VMEM((S // 2, D * C, N), BF16),
            dma((S,)), dma((S,)),
            *[dma((PARTS, S))] * 2,
            *[dma((PARTS, D))] * 4,
            *[dma((PARTS, S // 2))] * 8,
            *[dma((PARTS, D))] * 4,
            *[dma((PARTS, S // 2))] * 2,
            dma((3,)),
        ],
        compiler_params=pltpu.CompilerParams(
            collective_id=0, has_side_effects=True, vmem_limit_bytes=VMEM_LIMIT
        ),
    )(ordered.reshape(S, step, N), ids_all, rhs_cols, schur_inverse)

    interface_solution = values.reshape(S * half, N).astype(F32)
    group = math.gcd(NB, 4)
    interior = pl.pallas_call(
        back_kernel,
        grid=(NB // group,),
        in_specs=[
            pl.BlockSpec((1, 1, group * K), lambda i: (i, 0, 0)),
            full(slots, N),
            pl.BlockSpec((group, None, K, B), lambda i: (i, 1, 0, 0)),
            pl.BlockSpec((group, B, B), lambda i: (i, 0, 0)),
            pl.BlockSpec((group, B, N), lambda i: (i, 0, 0)),
        ],
        out_specs=pl.BlockSpec((group, B, N), lambda i: (i, 0, 0)),
        out_shape=jax.ShapeDtypeStruct((NB, B, N), BF16),
        compiler_params=pltpu.CompilerParams(vmem_limit_bytes=VMEM_LIMIT),
    )(place_c.reshape(NB // group, 1, group * K), picked.reshape(slots, N), coupling, inv_blocks, solved)
    return (interior.reshape(NB * B, N), interface_solution)


def solution(mesh):
    placed = (
        P(("sec", "dev"), None),
        P(("sec", "dev"), None),
        P(("sec", "dev"), None, None),
        P(("sec", "dev"), None, None, None),
        P(("sec", "dev"), None),
        P(("sec", "dev")),
        P(),
        P("dev", "sec"),
    )
    return jax.shard_map(
        shards,
        mesh=mesh,
        in_specs=placed,
        out_specs=(P(("sec", "dev"), None), P("dev", None)),
        check_vma=False,
    )
```
